256 devices in a mesh: dp: 32 (over z_hi, y, core), block: 8 (over x, z_lo).
Axes of the slice: x: 4, y: 4, z: 8 (z_hi: 4, z_lo: 2; z = z_hi * 2 + z_lo), core: 2. Of those that a mesh axis runs over, the one named last changes fastest.
Arguments:
- inputs: bfloat16 [8192, 8192], P('block', 'dp'), may hold values from -6 to 6
- grad_out: bfloat16 [8192, 8192], P('block', 'dp'), may hold values from -6 to 6
- up_left: bfloat16 [64, 128, 512], P('block'), may hold values from -0.5 to 0.5
- up_right: bfloat16 [64, 512, 512], P('block'), may hold values from -0.25 to 0.25
- down_left: bfloat16 [64, 512, 512], P('block'), may hold values from -0.25 to 0.25
- down_right: bfloat16 [64, 512, 128], P('block'), may hold values from -0.25 to 0.25
Outputs:
- grad_in: bfloat16 [8192, 8192], P('block', 'dp')
- grad_up_left: float32 [64, 128, 512], P('block', 'dp')
- grad_up_right: float32 [64, 512, 512], P('block', 'dp')
- grad_down_left: float32 [64, 512, 512], P('block', 'dp')
- grad_down_right: float32 [64, 512, 128], P('block', 'dp')
The draws below stay inside these ranges and needn't reach their ends.
All inputs are finite; a program needn't handle non-finite values.
Results may differ from the reference program's by a relative error of at most 0.0068.
Values may be sent and summed in bfloat16 or wider, within the bound.
No kernel may reach another device: no remote copies, remote signals or barrier semaphores. Data moves between devices by JAX's collectives and lax.ppermute only.
A program may use at most 128 MiB of HBM per device.

```python
import jax
import jax.numpy as jnp
from jax import lax

D = 8192
BLOCKS = 64
BLK_IN = 128
BLK_HID = 512
SPREAD = 8
TOK_DEV = 256
TOKENS = 8192
N_DP = 32


def shard_levels(stream_key, extent, split, low, top_value):
    factor_of = 1.0
    for position, shards_of in split:
        draws = jax.random.uniform(jax.random.fold_in(jax.random.fold_in(stream_key, 6), position), (shards_of,), jnp.float32, low / len(split), top_value / len(split))
        factor_of = factor_of * jnp.repeat(jnp.exp(draws), extent[position] // shards_of).reshape((-1,) + (1,) * (len(extent) - 1 - position))
    return factor_of


def bell_draw(rng, extent, scale, reach, split=(), kind=jnp.bfloat16):
    values = jax.random.normal(rng, extent, jnp.float32) * scale
    if len(split) > 0:
        values = shard_levels(rng, extent, split, -0.22, 0.18) * values
    return jnp.clip(values, min=-reach, max=reach).astype(kind)


def setup_inputs(seed: int = 0) -> dict:
    key_of = jax.random.split(jax.random.key(seed), 7)
    inputs = bell_draw(key_of[0], (D, TOKENS), 1.0, 6.0, ((0, 8), (1, 32)))
    grad_out = bell_draw(key_of[1], (D, TOKENS), 1.0, 6.0, ((0, 8), (1, 32)))
    up_left = bell_draw(key_of[2], (BLOCKS, BLK_IN, BLK_HID), BLK_IN ** -0.5, 0.5, ((0, 8),))
    up_right = bell_draw(key_of[3], (BLOCKS, BLK_HID, BLK_HID), BLK_HID ** -0.5, 0.25, ((0, 8),))
    down_left = bell_draw(key_of[4], (BLOCKS, BLK_HID, BLK_HID), BLK_HID ** -0.5, 0.25, ((0, 8),))
    down_right = bell_draw(key_of[5], (BLOCKS, BLK_HID, BLK_IN), BLK_HID ** -0.5, 0.25, ((0, 8),))
    return dict(inputs=inputs, grad_out=grad_out, up_left=up_left, up_right=up_right, down_left=down_left, down_right=down_right)


root_two_pi = 0.7978845608028654


def gelu_parts(pre):
    inner = root_two_pi * (pre + 0.044715 * pre * pre * pre)
    curve = jnp.tanh(inner)
    value = 0.5 * pre * (1.0 + curve)
    slope = 0.5 * (1.0 + curve) + 0.5 * pre * (1.0 - curve * curve) * root_two_pi * (1.0 + 3.0 * 0.044715 * pre * pre)
    return value, slope


def permute(array, width):
    return array.reshape(BLOCKS, BLOCKS, SPREAD, width).transpose(1, 0, 2, 3).reshape(BLOCKS, BLOCKS * SPREAD, width)


def reference(inputs, grad_out, up_left, up_right, down_left, down_right):
    single = jnp.float32
    half = jnp.bfloat16
    left_up = up_left.astype(single)
    right_up = up_right.astype(single)
    left_down = down_left.astype(single)
    right_down = down_right.astype(single)

    def step(carry, index):
        start = (index * TOK_DEV).astype(jnp.int32)
        feats = lax.dynamic_slice_in_dim(inputs, start, TOK_DEV, 1).reshape(BLOCKS, BLK_IN, TOK_DEV).astype(single)
        upstream = lax.dynamic_slice_in_dim(grad_out, start, TOK_DEV, 1).reshape(BLOCKS, BLK_IN, TOK_DEV).astype(single)
        mixed = jnp.einsum('bij,bit->bjt', left_up, feats).astype(half)
        spread_in = permute(mixed, TOK_DEV).astype(single)
        pre = jnp.einsum('cjm,cjt->cmt', right_up, spread_in)
        value, slope = gelu_parts(pre)
        hidden = value.astype(half).astype(single)
        lowered = jnp.einsum('cmj,cmt->cjt', left_down, hidden).astype(half)
        spread_down = permute(lowered, TOK_DEV).astype(single)
        g_right_down = jnp.einsum('djt,dot->djo', spread_down, upstream)
        back_down = jnp.einsum('djo,dot->djt', right_down, upstream).astype(half)
        returned = permute(back_down, TOK_DEV).astype(single)
        g_left_down = jnp.einsum('cmt,cjt->cmj', hidden, returned)
        back_hidden = jnp.einsum('cmj,cjt->cmt', left_down, returned)
        back_pre = (back_hidden * slope).astype(half).astype(single)
        g_right_up = jnp.einsum('cjt,cmt->cjm', spread_in, back_pre)
        back_mid = jnp.einsum('cjm,cmt->cjt', right_up, back_pre).astype(half)
        arrived = permute(back_mid, TOK_DEV).astype(single)
        g_left_up = jnp.einsum('bit,bjt->bij', feats, arrived)
        grad_block = jnp.einsum('bij,bjt->bit', left_up, arrived).astype(half).reshape(D, TOK_DEV)
        totals = (carry[0] + g_left_up, carry[1] + g_right_up, carry[2] + g_left_down, carry[3] + g_right_down)
        return totals, grad_block

    start_sums = (jnp.zeros((BLOCKS, BLK_IN, BLK_HID), single), jnp.zeros((BLOCKS, BLK_HID, BLK_HID), single),
                  jnp.zeros((BLOCKS, BLK_HID, BLK_HID), single), jnp.zeros((BLOCKS, BLK_HID, BLK_IN), single))
    totals, pieces = lax.scan(step, start_sums, jnp.arange(N_DP, dtype=jnp.int32))
    factor = float(TOKENS) ** -0.5
    grad_in = pieces.transpose(1, 0, 2).reshape(D, TOKENS)
    return (grad_in, totals[0] * factor, totals[1] * factor, totals[2] * factor, totals[3] * factor)
```

```python
import jax
import jax.numpy as jnp
from jax import lax
from jax.experimental import pallas as pl
from jax.experimental.pallas import tpu as pltpu
from jax.sharding import PartitionSpec as P

BLK_IN = 128
BLK_HID = 512
SPREAD = 8
LOCAL = 8
PEERS = 8
PAIR = 2 * SPREAD
ROWS = 16
HALF = LOCAL // 2

half = jnp.bfloat16
single = jnp.float32
root_two_pi = 0.7978845608028654

Z, Y, CORES = 4, 4, 2


def dp_perm(dz, dy, dc):
    pairs = []
    for z in range(Z):
        for y in range(Y):
            for c in range(CORES):
                source = (z * Y + y) * CORES + c
                target = ((z + dz) % Z * Y + (y + dy) % Y) * CORES + (c + dc) % CORES
                pairs.append((source, target))
    return pairs


def gelu_parts(pre):
    inner = root_two_pi * (pre + 0.044715 * pre * pre * pre)
    curve = jnp.tanh(inner)
    value = 0.5 * pre * (1.0 + curve)
    slope = 0.5 * (1.0 + curve) + 0.5 * pre * (1.0 - curve * curve) * root_two_pi * (
        1.0 + 3.0 * 0.044715 * pre * pre
    )
    return value, slope


def dot(left, right, over_left, over_right):
    return lax.dot_general(
        left, right, (((over_left,), (over_right,)), ((), ())), preferred_element_type=single
    )


def spread_pair(first, second):
    tokens = first.shape[-1]
    parts = [r.reshape(BLK_HID // SPREAD, SPREAD, tokens) for r in (first, second)]
    return jnp.concatenate(parts, axis=1).astype(half)


def call(kernel, grid, in_specs, out_specs, out_shape, scratch=(), flops=0, moved=0):
    return pl.pallas_call(
        kernel,
        grid_spec=pltpu.PrefetchScalarGridSpec(
            num_scalar_prefetch=1,
            grid=grid,
            in_specs=in_specs,
            out_specs=out_specs,
            scratch_shapes=list(scratch),
        ),
        out_shape=out_shape,
        compiler_params=pltpu.CompilerParams(vmem_limit_bytes=48 * 1024 * 1024),
        cost_estimate=pl.CostEstimate(flops=flops, bytes_accessed=moved, transcendentals=0),
    )


def first_kernel(me, x_ref, g_ref, up_ref, down_ref, one_ref, two_ref):
    ups, downs = [], []
    for i in range(2):
        rows = slice(i * BLK_IN, (i + 1) * BLK_IN)
        ups.append(dot(up_ref[i], x_ref[rows], 0, 0))
        downs.append(dot(down_ref[i], g_ref[rows], 1, 0))
    for slot, pair in enumerate((ups, downs)):
        spread = spread_pair(*pair).reshape(PEERS, 2, HALF, PAIR, -1)
        one_ref[:, slot] = spread[:, 0]
        two_ref[:, slot] = spread[:, 1]


def first_stage(me, inputs, grad_out, up_left, down_right):
    tokens = inputs.shape[1]
    shape = jax.ShapeDtypeStruct((PEERS, 2, HALF, LOCAL * SPREAD, tokens), half)
    out = pl.BlockSpec((PEERS, 2, HALF, PAIR, tokens), lambda p, me: (0, 0, 0, p, 0))
    return call(
        first_kernel,
        (LOCAL // 2,),
        [
            pl.BlockSpec((2 * BLK_IN, tokens), lambda p, me: (p, 0)),
            pl.BlockSpec((2 * BLK_IN, tokens), lambda p, me: (p, 0)),
            pl.BlockSpec((2, BLK_IN, BLK_HID), lambda p, me: (p, 0, 0)),
            pl.BlockSpec((2, BLK_HID, BLK_IN), lambda p, me: (p, 0, 0)),
        ],
        [out, out],
        [shape, shape],
        flops=4 * LOCAL * BLK_IN * BLK_HID * tokens,
        moved=7 << 20,
    )(me, inputs, grad_out, up_left, down_right)


def place(me, held, own_ref, other_ref, index):
    for ry in range(Y):
        for rz in range(Z):
            group = ((me[2] + rz) % Z * Y + (me[1] + ry) % Y) * CORES
            own_ref[(ry, rz) + index] = held[group + me[0]]
            other_ref[(ry, rz) + index] = held[group + 1 - me[0]]


def middle_kernel(me, got_ref, up_ref, down_ref, back_ref, own_ref, other_ref, held):
    lows, mids = [], []
    for i in range(2):
        v = got_ref[:, 0, i].reshape(BLK_HID, -1)
        f = got_ref[:, 1, i].reshape(BLK_HID, -1)
        up, down = up_ref[i], down_ref[i]
        value, slope = gelu_parts(dot(up, v, 0, 0))
        hidden = value.astype(half)
        lows.append(dot(down, hidden, 0, 0))
        held[0] = dot(hidden, f, 1, 1).astype(half).reshape(-1, ROWS, BLK_HID)
        place(me, held.at[0], own_ref, other_ref, (0, i))
        back = (dot(down, f, 1, 0) * slope).astype(half)
        mids.append(dot(up, back, 1, 0))
        held[1] = dot(v, back, 1, 1).astype(half).reshape(-1, ROWS, BLK_HID)
        place(me, held.at[1], own_ref, other_ref, (1, i))
    back_ref[:, 0] = spread_pair(*lows).reshape(PEERS, LOCAL, PAIR, -1)
    back_ref[:, 1] = spread_pair(*mids).reshape(PEERS, LOCAL, PAIR, -1)


def middle_stage(me, chunk, got, up_right, down_left):
    tokens = got.shape[-1]
    pairs = HALF // 2
    grads = jax.ShapeDtypeStruct((Y, Z, 2, HALF, ROWS, BLK_HID), half)
    grads_spec = pl.BlockSpec(
        (Y, Z, 2, 2, ROWS, BLK_HID), lambda p, me: (0, 0, 0, p, 0, 0)
    )
    weight = pl.BlockSpec((2, BLK_HID, BLK_HID), lambda p, me: (chunk * pairs + p, 0, 0))
    return call(
        middle_kernel,
        (pairs,),
        [
            pl.BlockSpec((PEERS, 2, 2, LOCAL * SPREAD, tokens), lambda p, me: (0, 0, p, 0, 0)),
            weight,
            weight,
        ],
        [
            pl.BlockSpec((PEERS, 2, LOCAL, PAIR, tokens), lambda p, me: (0, 0, 0, p, 0)),
            grads_spec,
            grads_spec,
        ],
        [
            jax.ShapeDtypeStruct((PEERS, 2, LOCAL, HALF * SPREAD, tokens), half),
            grads,
            grads,
        ],
        scratch=[pltpu.VMEM((2, BLK_HID // ROWS, ROWS, BLK_HID), half)],
        flops=12 * HALF * BLK_HID * BLK_HID * tokens,
        moved=16 << 20,
    )(me, got, up_right, down_left)


def last_kernel(me, one_ref, two_ref, x_ref, g_ref, up_ref, in_ref, own_ref, other_ref, held, held_down):
    tokens = x_ref.shape[-1]
    rows4 = BLK_IN // (Z * Y * CORES)
    evens, odds = [], []
    for i in range(4):
        rows = slice(i * BLK_IN, (i + 1) * BLK_IN)
        a2, du = [
            jnp.concatenate([one_ref[:, slot, i], two_ref[:, slot, i]], axis=1).reshape(
                BLK_HID, tokens
            )
            for slot in range(2)
        ]
        in_ref[rows] = dot(up_ref[i], du, 1, 0).astype(half)
        left = dot(x_ref[rows], du, 1, 1).reshape(-1, 2 * rows4, BLK_HID)
        evens.append(left[:, :rows4])
        odds.append(left[:, rows4:])
        right = dot(a2, g_ref[rows], 1, 1).astype(half)
        held_down[:, :, i * BLK_IN : (i + 1) * BLK_IN] = right.reshape(-1, ROWS, BLK_IN)
    for core, parts in enumerate((evens, odds)):
        held[core] = jnp.concatenate(parts, axis=1).astype(half)
    for ry in range(Y):
        for rz in range(Z):
            chip = (me[2] + rz) % Z * Y + (me[1] + ry) % Y
            own_ref[ry, rz, 0, 0] = held[me[0], chip]
            other_ref[ry, rz, 0, 0] = held[1 - me[0], chip]
            own_ref[ry, rz, 1, 0] = held_down[chip * CORES + me[0]]
            other_ref[ry, rz, 1, 0] = held_down[chip * CORES + 1 - me[0]]


def last_stage(me, one, two, inputs, grad_out, up_left):
    tokens = inputs.shape[1]
    groups = LOCAL // 4
    grads = jax.ShapeDtypeStruct((Y, Z, 2, groups, ROWS, BLK_HID), half)
    grads_spec = pl.BlockSpec((Y, Z, 2, 1, ROWS, BLK_HID), lambda p, me: (0, 0, 0, p, 0, 0))
    got = pl.BlockSpec((PEERS, 2, 4, HALF * SPREAD, tokens), lambda p, me: (0, 0, p, 0, 0))
    feats = pl.BlockSpec((4 * BLK_IN, tokens), lambda p, me: (p, 0))
    return call(
        last_kernel,
        (groups,),
        [got, got, feats, feats, pl.BlockSpec((4, BLK_IN, BLK_HID), lambda p, me: (p, 0, 0))],
        [feats, grads_spec, grads_spec],
        [jax.ShapeDtypeStruct(inputs.shape, half), grads, grads],
        scratch=[
            pltpu.VMEM((CORES, Z * Y, ROWS, BLK_HID), half),
            pltpu.VMEM((Z * Y * CORES, ROWS, BLK_HID), half),
        ],
        flops=6 * LOCAL * BLK_IN * BLK_HID * tokens,
        moved=12 << 20,
    )(me, one, two, inputs, grad_out, up_left)


def core_kernel(me, own_ref, got_ref, keep_ref, *send_refs):
    keep_ref[...] = own_ref[0].astype(single) + got_ref[0].astype(single)
    for r, send in enumerate(send_refs):
        send[...] = (own_ref[r + 1].astype(single) + got_ref[r + 1].astype(single)).astype(half)


def core_sum(me, own, got):
    n = own.shape[2]
    whole = pl.BlockSpec((Y, 1, n, ROWS, BLK_HID), lambda p, me: (0, p, 0, 0, 0))
    part = pl.BlockSpec((1, n, ROWS, BLK_HID), lambda p, me: (p, 0, 0, 0))
    shape = (Z, n, ROWS, BLK_HID)
    return call(
        core_kernel,
        (Z,),
        [whole, whole],
        [part] * Y,
        [jax.ShapeDtypeStruct(shape, single)] + [jax.ShapeDtypeStruct(shape, half)] * (Y - 1),
        flops=own.size,
        moved=own.size * 6,
    )(me, own, got)


def line_kernel(me, keep_ref, a_ref, b_ref, c_ref, rest_ref, *send_refs):
    for r in range(Z):
        total = keep_ref[r] + a_ref[r].astype(single)
        total = total + (b_ref[r].astype(single) + c_ref[r].astype(single))
        if r == 0:
            rest_ref[...] = total
        else:
            send_refs[r - 1][...] = total.astype(half)


def line_sum(me, keep, got):
    n = keep.shape[1]
    steps = 2
    whole = pl.BlockSpec((Z, n // steps, ROWS, BLK_HID), lambda p, me: (0, p, 0, 0))
    part = pl.BlockSpec((n // steps, ROWS, BLK_HID), lambda p, me: (p, 0, 0))
    shape = (n, ROWS, BLK_HID)
    return call(
        line_kernel,
        (steps,),
        [whole] * Y,
        [part] * Z,
        [jax.ShapeDtypeStruct(shape, single)] + [jax.ShapeDtypeStruct(shape, half)] * (Z - 1),
        flops=keep.size * 3,
        moved=keep.size * 12,
    )(me, keep, *got)


def end_kernel(factor, me, keep_ref, a_ref, b_ref, c_ref, out_ref):
    total = keep_ref[...] + a_ref[...].astype(single)
    out_ref[...] = factor * (total + (b_ref[...].astype(single) + c_ref[...].astype(single)))


def end_sum(me, factor, keep, got):
    def kernel(*refs):
        end_kernel(factor, *refs)

    whole = pl.BlockSpec(keep.shape, lambda p, me: (0, 0, 0))
    return call(
        kernel,
        (1,),
        [whole] * Z,
        whole,
        jax.ShapeDtypeStruct(keep.shape, single),
        flops=keep.size * 3,
        moved=keep.size * 14,
    )(me, keep, *got)


def reduce_rows(me, factor, own, other):
    shape = own.shape[2:]
    flat = (Y, Z, -1, ROWS, BLK_HID)
    got = lax.ppermute(other.reshape(flat), "dp", dp_perm(0, 0, 1))
    keep, *sends = core_sum(me, own.reshape(flat), got)
    got = [lax.ppermute(s, "dp", dp_perm(0, r + 1, 0)) for r, s in enumerate(sends)]
    keep, *sends = line_sum(me, keep, got)
    got = [lax.ppermute(s, "dp", dp_perm(r + 1, 0, 0)) for r, s in enumerate(sends)]
    return end_sum(me, factor, keep, got).reshape(shape)


def exchange(array):
    return lax.all_to_all(array, "block", split_axis=0, concat_axis=0, tiled=True)


def shards(inputs, grad_out, up_left, up_right, down_left, down_right):
    tokens = inputs.shape[1]
    factor = float(tokens * lax.axis_size("dp")) ** (-0.5)
    dp = lax.axis_index("dp")
    me = jnp.stack([dp % CORES, dp // CORES % Y, dp // (CORES * Y)]).astype(jnp.int32)

    one, two = first_stage(me, inputs, grad_out, up_left, down_right)
    backs, grads = [], []
    for chunk, sent in enumerate((one, two)):
        back, own, other = middle_stage(me, chunk, exchange(sent), up_right, down_left)
        backs.append(exchange(back))
        grads.append(reduce_rows(me, factor, own, other))
    grad_in, own, other = last_stage(me, *backs, inputs, grad_out, up_left)
    outer = reduce_rows(me, factor, own, other)

    grad_left_down, grad_right_up = [
        jnp.concatenate([g[k] for g in grads], axis=0) for k in range(2)
    ]
    rows4 = BLK_IN // (Z * Y * CORES)
    grad_left_up = outer[0].reshape(LOCAL, rows4, BLK_HID)
    grad_right_down = (
        outer[1].reshape(LOCAL // 4, ROWS, 4, BLK_IN).transpose(0, 2, 1, 3).reshape(LOCAL, ROWS, BLK_IN)
    )
    return grad_in, grad_left_up, grad_right_up, grad_left_down, grad_right_down


def solution(mesh):
    in_specs = (
        P("block", "dp"),
        P("block", "dp"),
        P("block", None, None),
        P("block", None, None),
        P("block", None, None),
        P("block", None, None),
    )
    out_specs = (
        P("block", "dp"),
        P("block", "dp", None),
        P("block", "dp", None),
        P("block", "dp", None),
        P("block", "dp", None),
    )
    return jax.shard_map(shards, mesh=mesh, in_specs=in_specs, out_specs=out_specs, check_vma=False)
```

```python
import jax
import jax.numpy as jnp
from jax import lax
from jax.experimental import pallas as pl
from jax.experimental.pallas import tpu as pltpu
from jax.sharding import PartitionSpec as P

BLK_IN = 128
BLK_HID = 512
SPREAD = 8
LOCAL = 8
PEERS = 8
PAIR = 2 * SPREAD
VMEM_LIMIT = 63 * 1024 * 1024
ROWS = 16
PAIRS = LOCAL // 2
CHUNKS = (1, 3)

half = jnp.bfloat16
single = jnp.float32
root_two_pi = 0.7978845608028654

Z, Y, CORES = 4, 4, 2


def dp_perm(dz, dy, dc):
    pairs = []
    for z in range(Z):
        for y in range(Y):
            for c in range(CORES):
                source = (z * Y + y) * CORES + c
                target = ((z + dz) % Z * Y + (y + dy) % Y) * CORES + (c + dc) % CORES
                pairs.append((source, target))
    return pairs


def gelu_parts(pre):
    inner = root_two_pi * (pre + 0.044715 * pre * pre * pre)
    curve = jnp.tanh(inner)
    value = 0.5 * pre * (1.0 + curve)
    slope = 0.5 * (1.0 + curve) + 0.5 * pre * (1.0 - curve * curve) * root_two_pi * (
        1.0 + 3.0 * 0.044715 * pre * pre
    )
    return value, slope


def dot(left, right, over_left, over_right):
    return lax.dot_general(
        left, right, (((over_left,), (over_right,)), ((), ())), preferred_element_type=single
    )


def spread_pair(first, second):
    tokens = first.shape[-1]
    parts = [r.reshape(BLK_HID // SPREAD, SPREAD, tokens) for r in (first, second)]
    return jnp.concatenate(parts, axis=1).astype(half)


def call(
    kernel, grid, in_specs, out_specs, out_shape, scratch=(), after=(), carry=()
):
    first = 1 + len(in_specs)
    extra = len(after) + len(carry)
    outs = len(out_specs)
    untouched = pl.BlockSpec(memory_space=pl.ANY)

    def body(*refs):
        ends = first + extra + outs
        kernel(*refs[:first], *refs[first + extra : ends], *refs[ends + len(carry) :])

    run = pl.pallas_call(
        body,
        grid_spec=pltpu.PrefetchScalarGridSpec(
            num_scalar_prefetch=1,
            grid=grid,
            in_specs=list(in_specs) + [untouched] * extra,
            out_specs=list(out_specs) + [untouched] * len(carry),
            scratch_shapes=list(scratch),
        ),
        out_shape=list(out_shape) + [jax.ShapeDtypeStruct(c.shape, c.dtype) for c in carry],
        input_output_aliases={first + len(after) + i: outs + i for i in range(len(carry))},
        compiler_params=pltpu.CompilerParams(vmem_limit_bytes=VMEM_LIMIT),
    )
    return lambda *operands: run(*operands, *after, *carry)


def first_kernel(me, x_ref, g_ref, up_ref, down_ref, *out_refs):
    ups, downs = [], []
    for i in range(2):
        rows = slice(i * BLK_IN, (i + 1) * BLK_IN)
        ups.append(dot(up_ref[i], x_ref[rows], 0, 0))
        downs.append(dot(down_ref[i], g_ref[rows], 1, 0))
    for slot, pair in enumerate((ups, downs)):
        spread = spread_pair(*pair).reshape(PEERS, LOCAL, PAIR, -1)
        start = 0
        for pairs, out in zip(CHUNKS, out_refs):
            out[:, slot] = spread[:, start : start + 2 * pairs]
            start += 2 * pairs


def first_stage(me, inputs, grad_out, up_left, down_right):
    tokens = inputs.shape[1]
    return call(
        first_kernel,
        (PAIRS,),
        [
            pl.BlockSpec((2 * BLK_IN, tokens), lambda p, me: (p, 0)),
            pl.BlockSpec((2 * BLK_IN, tokens), lambda p, me: (p, 0)),
            pl.BlockSpec((2, BLK_IN, BLK_HID), lambda p, me: (p, 0, 0)),
            pl.BlockSpec((2, BLK_HID, BLK_IN), lambda p, me: (p, 0, 0)),
        ],
        [
            pl.BlockSpec((PEERS, 2, 2 * n, PAIR, tokens), lambda p, me: (0, 0, 0, p, 0))
            for n in CHUNKS
        ],
        [
            jax.ShapeDtypeStruct((PEERS, 2, 2 * n, LOCAL * SPREAD, tokens), half) for n in CHUNKS
        ],
    )(me, inputs, grad_out, up_left, down_right)


def place(me, held, own_ref, other_ref, index):
    for ry in range(Y):
        for rz in range(Z):
            group = ((me[2] + rz) % Z * Y + (me[1] + ry) % Y) * CORES
            own_ref[(ry, rz) + index] = held[group + me[0]]
            other_ref[(ry, rz) + index] = held[group + 1 - me[0]]


def middle_kernel(me, got_ref, up_ref, down_ref, back_ref, own_ref, other_ref, held):
    lows, mids = [], []
    for i in range(2):
        v = got_ref[:, 0, i].reshape(BLK_HID, -1)
        f = got_ref[:, 1, i].reshape(BLK_HID, -1)
        up, down = up_ref[i], down_ref[i]
        value, slope = gelu_parts(dot(up, v, 0, 0))
        hidden = value.astype(half)
        lows.append(dot(down, hidden, 0, 0))
        held[0] = dot(hidden, f, 1, 1).astype(half).reshape(-1, ROWS, BLK_HID)
        place(me, held.at[0], own_ref, other_ref, (0, i))
        back = (dot(down, f, 1, 0) * slope).astype(half)
        mids.append(dot(up, back, 1, 0))
        held[1] = dot(v, back, 1, 1).astype(half).reshape(-1, ROWS, BLK_HID)
        place(me, held.at[1], own_ref, other_ref, (1, i))
    back_ref[:, 0] = spread_pair(*lows).reshape(PEERS, LOCAL, PAIR, -1)
    back_ref[:, 1] = spread_pair(*mids).reshape(PEERS, LOCAL, PAIR, -1)


def middle_stage(me, chunk, got, up_right, down_left, **order):
    tokens = got.shape[-1]
    pairs = CHUNKS[chunk]
    start = sum(CHUNKS[:chunk])
    grads = jax.ShapeDtypeStruct((Y, Z, 2, 2 * pairs, ROWS, BLK_HID), half)
    grads_spec = pl.BlockSpec((Y, Z, 2, 2, ROWS, BLK_HID), lambda p, me: (0, 0, 0, p, 0, 0))
    weight = pl.BlockSpec((2, BLK_HID, BLK_HID), lambda p, me: (start + p, 0, 0))
    return call(
        middle_kernel,
        (pairs,),
        [
            pl.BlockSpec((PEERS, 2, 2, LOCAL * SPREAD, tokens), lambda p, me: (0, 0, p, 0, 0)),
            weight,
            weight,
        ],
        [
            pl.BlockSpec((PEERS, 2, LOCAL, PAIR, tokens), lambda p, me: (0, 0, 0, p, 0)),
            grads_spec,
            grads_spec,
        ],
        [
            jax.ShapeDtypeStruct((PEERS, 2, LOCAL, pairs * PAIR, tokens), half),
            grads,
            grads,
        ],
        scratch=[pltpu.VMEM((2, BLK_HID // ROWS, ROWS, BLK_HID), half)],
        **order,
    )(me, got, up_right, down_left)


def features(one_ref, two_ref, slot, i):
    both = jnp.concatenate([one_ref[:, slot, i], two_ref[:, slot, i]], axis=1)
    return both.reshape(BLK_HID, -1)


def outer_kernel(me, one_ref, two_ref, x_ref, g_ref, own_ref, other_ref, held, held_down):
    rows4 = BLK_IN // (Z * Y * CORES)
    evens, odds = [], []
    for i in range(4):
        rows = slice(i * BLK_IN, (i + 1) * BLK_IN)
        left = dot(x_ref[rows], features(one_ref, two_ref, 1, i), 1, 1)
        left = left.reshape(-1, 2 * rows4, BLK_HID)
        evens.append(left[:, :rows4])
        odds.append(left[:, rows4:])
        right = dot(features(one_ref, two_ref, 0, i), g_ref[rows], 1, 1).astype(half)
        held_down[:, :, i * BLK_IN : (i + 1) * BLK_IN] = right.reshape(-1, ROWS, BLK_IN)
    for core, parts in enumerate((evens, odds)):
        held[core] = jnp.concatenate(parts, axis=1).astype(half)
    for y in range(Y):
        for z in range(Z):
            chip = z * Y + y
            own_ref[y, z, 0, 0] = held[me[0], chip]
            other_ref[y, z, 0, 0] = held[1 - me[0], chip]
            own_ref[y, z, 1, 0] = held_down[chip * CORES + me[0]]
            other_ref[y, z, 1, 0] = held_down[chip * CORES + 1 - me[0]]


def got_specs(tokens):
    return [
        pl.BlockSpec((PEERS, 2, 4, n * PAIR, tokens), lambda p, me: (0, 0, p, 0, 0)) for n in CHUNKS
    ]


def outer_stage(me, one, two, inputs, grad_out, **order):
    tokens = inputs.shape[1]
    groups = LOCAL // 4
    grads = jax.ShapeDtypeStruct((Y, Z, 2, groups, ROWS, BLK_HID), half)
    grads_spec = pl.BlockSpec((Y, Z, 2, 1, ROWS, BLK_HID), lambda p, me: (0, 0, 0, p, 0, 0))
    feats = pl.BlockSpec((4 * BLK_IN, tokens), lambda p, me: (p, 0))
    return call(
        outer_kernel,
        (groups,),
        got_specs(tokens) + [feats, feats],
        [grads_spec, grads_spec],
        [grads, grads],
        scratch=[
            pltpu.VMEM((CORES, Z * Y, ROWS, BLK_HID), half),
            pltpu.VMEM((Z * Y * CORES, ROWS, BLK_HID), half),
        ],
        **order,
    )(me, one, two, inputs, grad_out)


def back_kernel(me, one_ref, two_ref, up_ref, in_ref):
    for i in range(4):
        rows = slice(i * BLK_IN, (i + 1) * BLK_IN)
        in_ref[rows] = dot(up_ref[i], features(one_ref, two_ref, 1, i), 1, 0).astype(half)


def back_stage(me, one, two, up_left, **order):
    tokens = one.shape[-1]
    return call(
        back_kernel,
        (LOCAL // 4,),
        got_specs(tokens) + [pl.BlockSpec((4, BLK_IN, BLK_HID), lambda p, me: (p, 0, 0))],
        [pl.BlockSpec((4 * BLK_IN, tokens), lambda p, me: (p, 0))],
        [jax.ShapeDtypeStruct((LOCAL * BLK_IN, tokens), half)],
        **order,
    )(me, one, two, up_left)


def flat(array):
    return array.reshape(Y, Z, -1, ROWS, BLK_HID)


def core_step(own, other):
    own = flat(own)
    got = lax.ppermute(flat(other), "dp", dp_perm(0, 0, 1))
    sums = [own[r].astype(single) + got[r].astype(single) for r in range(Y)]
    return sums[0], *[total.astype(half) for total in sums[1:]]


def gate(me, arrays, after=()):
    def kernel(me, out_ref):
        out_ref[...] = jnp.zeros_like(out_ref)

    return call(
        kernel,
        (1,),
        [],
        [pl.BlockSpec((8, 128), lambda p, me: (0, 0))],
        [jax.ShapeDtypeStruct((8, 128), single)],
        after=after,
        carry=arrays,
    )(me)[1:]


def add(keep, got):
    return keep + sum(part.astype(single) for part in got)


def line_step(keep, *sends):
    got = [lax.ppermute(s, "dp", dp_perm(0, r + 1, 0)) for r, s in enumerate(sends)]
    sums = [add(keep[r], [part[r] for part in got]) for r in range(Z)]
    return sums[0], *[total.astype(half) for total in sums[1:]]


def end_moves(keep, *sends):
    return [lax.ppermute(s, "dp", dp_perm(r + 1, 0, 0)) for r, s in enumerate(sends)]


def exchange(array):
    return lax.all_to_all(array, "block", split_axis=0, concat_axis=0, tiled=True)


def line_groups(of_y):
    spans = (Z, CORES) if of_y else (Y, CORES)
    groups = []
    for i in range(spans[0]):
        for c in range(CORES):
            lines = [(i, y) if of_y else (z, i) for y, z in zip(range(Y), range(Z))]
            groups.append([(z * Y + y) * CORES + c for z, y in lines])
    return groups


def share(array, of_y):
    got = lax.all_to_all(
        array, "dp", split_axis=0, concat_axis=0, tiled=True, axis_index_groups=line_groups(of_y)
    )
    return got.astype(single).sum(axis=0)


def shards(inputs, grad_out, up_left, up_right, down_left, down_right):
    tokens = inputs.shape[1]
    factor = float(tokens * lax.axis_size("dp")) ** (-0.5)
    dp = lax.axis_index("dp")
    me = jnp.stack([dp % CORES, dp // CORES % Y, dp // (CORES * Y)]).astype(jnp.int32)

    one, two = first_stage(me, inputs, grad_out, up_left, down_right)
    back1, own, other = middle_stage(me, 0, exchange(one), up_right, down_left)
    sums1 = line_step(*core_step(own, other))
    (back1,) = gate(me, [back1], sums1)
    back2, own, other, *sums1 = middle_stage(
        me, 1, exchange(two), up_right, down_left, carry=sums1
    )
    sums2 = core_step(own, other)
    back1, back2 = exchange(back1), exchange(back2)
    own, other = outer_stage(me, back1, back2, inputs, grad_out)
    outer = flat(own).astype(single)
    outer = outer + lax.ppermute(flat(other), "dp", dp_perm(0, 0, 1)).astype(single)
    sums2 = line_step(*sums2)
    got1 = end_moves(*sums1)
    outer, *sums2 = gate(me, [outer.astype(half), *sums2], got1)
    got2 = end_moves(*sums2)
    (grad_in,) = back_stage(me, back1, back2, up_left, after=(outer,))
    outer = share(share(outer, True).astype(half), False) * factor
    outer = outer.reshape(2, -1, ROWS, BLK_HID)
    grads = [
        (factor * add(sums[0], got)).reshape(2, -1, ROWS, BLK_HID)
        for sums, got in ((sums1, got1), (sums2, got2))
    ]
    grad_left_down, grad_right_up = [
        jnp.concatenate([g[k] for g in grads], axis=0) for k in range(2)
    ]
    rows4 = BLK_IN // (Z * Y * CORES)
    grad_left_up = outer[0].reshape(LOCAL, rows4, BLK_HID)
    grad_right_down = (
        outer[1].reshape(LOCAL // 4, ROWS, 4, BLK_IN).transpose(0, 2, 1, 3).reshape(LOCAL, ROWS, BLK_IN)
    )
    return grad_in, grad_left_up, grad_right_up, grad_left_down, grad_right_down


def solution(mesh):
    in_specs = (
        P("block", "dp"),
        P("block", "dp"),
        P("block", None, None),
        P("block", None, None),
        P("block", None, None),
        P("block", None, None),
    )
    out_specs = (
        P("block", "dp"),
        P("block", "dp", None),
        P("block", "dp", None),
        P("block", "dp", None),
        P("block", "dp", None),
    )
    return jax.shard_map(shards, mesh=mesh, in_specs=in_specs, out_specs=out_specs, check_vma=False)
```

```python
import jax
import jax.numpy as jnp
from jax import lax
from jax.experimental import pallas as pl
from jax.experimental.pallas import tpu as pltpu
from jax.sharding import PartitionSpec as P

BLK_IN = 128
BLK_HID = 512
SPREAD = 8
LOCAL = 8
PEERS = 8
PAIR = 2 * SPREAD
VMEM_LIMIT = 63 * 1024 * 1024
ROWS = 16
PAIRS = LOCAL // 2
CHUNKS = (1, 3)

half = jnp.bfloat16
single = jnp.float32
root_two_pi = 0.7978845608028654

Z, Y, CORES = 4, 4, 2


def dp_perm(dz, dy, dc):
    pairs = []
    for z in range(Z):
        for y in range(Y):
            for c in range(CORES):
                source = (z * Y + y) * CORES + c
                target = ((z + dz) % Z * Y + (y + dy) % Y) * CORES + (c + dc) % CORES
                pairs.append((source, target))
    return pairs


def gelu_parts(pre):
    inner = root_two_pi * (pre + 0.044715 * pre * pre * pre)
    curve = jnp.tanh(inner)
    value = 0.5 * pre * (1.0 + curve)
    slope = 0.5 * (1.0 + curve) + 0.5 * pre * (1.0 - curve * curve) * root_two_pi * (
        1.0 + 3.0 * 0.044715 * pre * pre
    )
    return value, slope


def dot(left, right, over_left, over_right):
    return lax.dot_general(
        left, right, (((over_left,), (over_right,)), ((), ())), preferred_element_type=single
    )


def spread_pair(first, second):
    tokens = first.shape[-1]
    parts = [r.reshape(BLK_HID // SPREAD, SPREAD, tokens) for r in (first, second)]
    return jnp.concatenate(parts, axis=1).astype(half)


def position():
    dp = lax.axis_index("dp")
    return lax.rem(dp, CORES), lax.rem(lax.div(dp, CORES), Y), lax.div(dp, CORES * Y)


def call(
    kernel, grid, in_specs, out_specs, out_shape, scratch=(), after=(), carry=(), vmem=VMEM_LIMIT
):
    first = len(in_specs)
    extra = len(after) + len(carry)
    outs = len(out_specs)
    untouched = pl.BlockSpec(memory_space=pl.ANY)

    def body(*refs):
        ends = first + extra + outs
        kernel(position(), *refs[:first], *refs[first + extra : ends], *refs[ends + len(carry) :])

    run = pl.pallas_call(
        body,
        grid=grid,
        in_specs=list(in_specs) + [untouched] * extra,
        out_specs=list(out_specs) + [untouched] * len(carry),
        scratch_shapes=list(scratch),
        out_shape=list(out_shape) + [jax.ShapeDtypeStruct(c.shape, c.dtype) for c in carry],
        input_output_aliases={first + len(after) + i: outs + i for i in range(len(carry))},
        compiler_params=pltpu.CompilerParams(vmem_limit_bytes=vmem),
    )
    return lambda *operands: run(*operands, *after, *carry)


def first_kernel(chunk, x_ref, g_ref, up_ref, down_ref, out_ref):
    start = 2 * sum(CHUNKS[:chunk])
    for pair in range(2):
        ups, downs = [], []
        for i in (2 * pair, 2 * pair + 1):
            rows = slice(i * BLK_IN, (i + 1) * BLK_IN)
            ups.append(dot(up_ref[i], x_ref[rows], 0, 0))
            downs.append(dot(down_ref[i], g_ref[rows], 1, 0))
        where = slice(pair * PAIR, (pair + 1) * PAIR)
        for slot, both in enumerate((ups, downs)):
            spread = spread_pair(*both).reshape(PEERS, LOCAL, PAIR, -1)
            out_ref[:, slot, :, where] = spread[:, start : start + 2 * CHUNKS[chunk]]


def first_stage(chunk, inputs, grad_out, up_left, down_right, **order):
    tokens = inputs.shape[1]
    n = CHUNKS[chunk]

    def kernel(me, *refs):
        first_kernel(chunk, *refs)

    (out,) = call(
        kernel,
        (PAIRS // 2,),
        [
            pl.BlockSpec((4 * BLK_IN, tokens), lambda p: (p, 0)),
            pl.BlockSpec((4 * BLK_IN, tokens), lambda p: (p, 0)),
            pl.BlockSpec((4, BLK_IN, BLK_HID), lambda p: (p, 0, 0)),
            pl.BlockSpec((4, BLK_HID, BLK_IN), lambda p: (p, 0, 0)),
        ],
        [pl.BlockSpec((PEERS, 2, 2 * n, 2 * PAIR, tokens), lambda p: (0, 0, 0, p, 0))],
        [jax.ShapeDtypeStruct((PEERS, 2, 2 * n, LOCAL * SPREAD, tokens), half)],
        **order,
    )(inputs, grad_out, up_left, down_right)
    return out


def place(me, held, own_ref, other_ref, index):
    for ry in range(Y):
        for rz in range(Z):
            group = (lax.rem(me[2] + rz, Z) * Y + lax.rem(me[1] + ry, Y)) * CORES
            own_ref[(ry, rz) + index] = held[group + me[0]]
            other_ref[(ry, rz) + index] = held[group + 1 - me[0]]


def middle_kernel(me, got_ref, up_ref, down_ref, back_ref, own_ref, other_ref, held):
    lows, mids = [], []
    for i in range(2):
        v = got_ref[:, 0, i].reshape(BLK_HID, -1)
        f = got_ref[:, 1, i].reshape(BLK_HID, -1)
        up, down = up_ref[i], down_ref[i]
        value, slope = gelu_parts(dot(up, v, 0, 0))
        hidden = value.astype(half)
        lows.append(dot(down, hidden, 0, 0))
        held[0] = dot(hidden, f, 1, 1).astype(half).reshape(-1, ROWS, BLK_HID)
        place(me, held.at[0], own_ref, other_ref, (0, i))
        back = (dot(down, f, 1, 0) * slope).astype(half)
        mids.append(dot(up, back, 1, 0))
        held[1] = dot(v, back, 1, 1).astype(half).reshape(-1, ROWS, BLK_HID)
        place(me, held.at[1], own_ref, other_ref, (1, i))
    back_ref[:, 0] = spread_pair(*lows).reshape(PEERS, LOCAL, PAIR, -1)
    back_ref[:, 1] = spread_pair(*mids).reshape(PEERS, LOCAL, PAIR, -1)


def middle_stage(chunk, got, up_right, down_left, **order):
    tokens = got.shape[-1]
    pairs = CHUNKS[chunk]
    start = sum(CHUNKS[:chunk])
    grads = jax.ShapeDtypeStruct((Y, Z, 2, 2 * pairs, ROWS, BLK_HID), half)
    grads_spec = pl.BlockSpec((Y, Z, 2, 2, ROWS, BLK_HID), lambda p: (0, 0, 0, p, 0, 0))
    weight = pl.BlockSpec((2, BLK_HID, BLK_HID), lambda p: (start + p, 0, 0))
    return call(
        middle_kernel,
        (pairs,),
        [
            pl.BlockSpec((PEERS, 2, 2, LOCAL * SPREAD, tokens), lambda p: (0, 0, p, 0, 0)),
            weight,
            weight,
        ],
        [
            pl.BlockSpec((PEERS, 2, LOCAL, PAIR, tokens), lambda p: (0, 0, 0, p, 0)),
            grads_spec,
            grads_spec,
        ],
        [
            jax.ShapeDtypeStruct((PEERS, 2, LOCAL, pairs * PAIR, tokens), half),
            grads,
            grads,
        ],
        scratch=[pltpu.VMEM((2, BLK_HID // ROWS, ROWS, BLK_HID), half)],
        **order,
    )(got, up_right, down_left)


def features(one_ref, two_ref, slot, i):
    both = jnp.concatenate([one_ref[:, slot, i], two_ref[:, slot, i]], axis=1)
    return both.reshape(BLK_HID, -1)


def outer_kernel(me, one_ref, two_ref, x_ref, g_ref, own_ref, other_ref, held, held_down):
    rows4 = BLK_IN // (Z * Y * CORES)
    evens, odds = [], []
    for i in range(4):
        rows = slice(i * BLK_IN, (i + 1) * BLK_IN)
        left = dot(x_ref[rows], features(one_ref, two_ref, 1, i), 1, 1)
        left = left.reshape(-1, 2 * rows4, BLK_HID)
        evens.append(left[:, :rows4])
        odds.append(left[:, rows4:])
        right = dot(features(one_ref, two_ref, 0, i), g_ref[rows], 1, 1).astype(half)
        held_down[:, :, i * BLK_IN : (i + 1) * BLK_IN] = right.reshape(-1, ROWS, BLK_IN)
    for core, parts in enumerate((evens, odds)):
        held[core] = jnp.concatenate(parts, axis=1).astype(half)
    for ry in range(Y):
        for z in range(Z):
            chip = z * Y + lax.rem(me[1] + ry, Y)
            own_ref[ry, z, 0, 0] = held[me[0], chip]
            other_ref[ry, z, 0, 0] = held[1 - me[0], chip]
            own_ref[ry, z, 1, 0] = held_down[chip * CORES + me[0]]
            other_ref[ry, z, 1, 0] = held_down[chip * CORES + 1 - me[0]]


def got_specs(tokens):
    return [
        pl.BlockSpec((PEERS, 2, 4, n * PAIR, tokens), lambda p: (0, 0, p, 0, 0)) for n in CHUNKS
    ]


def outer_stage(one, two, inputs, grad_out, **order):
    tokens = inputs.shape[1]
    groups = LOCAL // 4
    grads = jax.ShapeDtypeStruct((Y, Z, 2, groups, ROWS, BLK_HID), half)
    grads_spec = pl.BlockSpec((Y, Z, 2, 1, ROWS, BLK_HID), lambda p: (0, 0, 0, p, 0, 0))
    feats = pl.BlockSpec((4 * BLK_IN, tokens), lambda p: (p, 0))
    return call(
        outer_kernel,
        (groups,),
        got_specs(tokens) + [feats, feats],
        [grads_spec, grads_spec],
        [grads, grads],
        scratch=[
            pltpu.VMEM((CORES, Z * Y, ROWS, BLK_HID), half),
            pltpu.VMEM((Z * Y * CORES, ROWS, BLK_HID), half),
        ],
        **order,
    )(one, two, inputs, grad_out)


def back_kernel(me, one_ref, two_ref, up_ref, in_ref):
    for i in range(4):
        rows = slice(i * BLK_IN, (i + 1) * BLK_IN)
        in_ref[rows] = dot(up_ref[i], features(one_ref, two_ref, 1, i), 1, 0).astype(half)


def back_stage(one, two, up_left, **order):
    tokens = one.shape[-1]
    return call(
        back_kernel,
        (LOCAL // 4,),
        got_specs(tokens) + [pl.BlockSpec((4, BLK_IN, BLK_HID), lambda p: (p, 0, 0))],
        [pl.BlockSpec((4 * BLK_IN, tokens), lambda p: (p, 0))],
        [jax.ShapeDtypeStruct((LOCAL * BLK_IN, tokens), half)],
        **order,
    )(one, two, up_left)


def flat(array):
    return array.reshape(Y, Z, -1, ROWS, BLK_HID)


def core_step(own, other):
    own = flat(own)
    got = lax.ppermute(flat(other), "dp", dp_perm(0, 0, 1))
    sums = [own[r].astype(single) + got[r].astype(single) for r in range(Y)]
    return sums[0], *[total.astype(half) for total in sums[1:]]


def gate(arrays, after=()):
    def kernel(me, out_ref):
        out_ref[...] = jnp.zeros_like(out_ref)

    return call(
        kernel,
        (1,),
        [],
        [pl.BlockSpec((8, 128), lambda p: (0, 0))],
        [jax.ShapeDtypeStruct((8, 128), single)],
        after=after,
        carry=arrays,
        vmem=1 << 20,
    )()[1:]


def add(keep, got):
    return keep + sum(part.astype(single) for part in got)


def line_step(keep, *sends):
    got = [lax.ppermute(s, "dp", dp_perm(0, r + 1, 0)) for r, s in enumerate(sends)]
    sums = [add(keep[r], [part[r] for part in got]) for r in range(Z)]
    return sums[0], *[total.astype(half) for total in sums[1:]]


def end_moves(keep, *sends):
    return [lax.ppermute(s, "dp", dp_perm(r + 1, 0, 0)) for r, s in enumerate(sends)]


def exchange(array):
    return lax.all_to_all(array, "block", split_axis=0, concat_axis=0, tiled=True)


def line_groups(of_y):
    spans = (Z, CORES) if of_y else (Y, CORES)
    groups = []
    for i in range(spans[0]):
        for c in range(CORES):
            lines = [(i, y) if of_y else (z, i) for y, z in zip(range(Y), range(Z))]
            groups.append([(z * Y + y) * CORES + c for z, y in lines])
    return groups


def share(array, of_y):
    got = lax.all_to_all(
        array, "dp", split_axis=0, concat_axis=0, tiled=True, axis_index_groups=line_groups(of_y)
    )
    return got.astype(single).sum(axis=0)


def shards(inputs, grad_out, up_left, up_right, down_left, down_right):
    tokens = inputs.shape[1]
    factor = float(tokens * lax.axis_size("dp")) ** (-0.5)

    operands = (inputs, grad_out, up_left, down_right)
    one = first_stage(0, *operands)
    two = first_stage(1, *operands, after=(one,))
    back1, own, other = middle_stage(0, exchange(one), up_right, down_left)
    sums1 = line_step(*core_step(own, other))
    (back1,) = gate([back1], sums1)
    back2, own, other, *sums1 = middle_stage(
        1, exchange(two), up_right, down_left, carry=sums1
    )
    sums2 = core_step(own, other)
    back1, back2 = exchange(back1), exchange(back2)
    got1 = end_moves(*sums1)
    own, other = outer_stage(back1, back2, inputs, grad_out, after=got1[::2])
    keep, *sends = core_step(own, other)
    gated = gate([*sends, *line_step(*sums2)], got1[1:2])
    sends, sums2 = gated[: len(sends)], gated[len(sends) :]
    outer = add(keep, [lax.ppermute(s, "dp", dp_perm(0, r + 1, 0)) for r, s in enumerate(sends)])
    got2 = end_moves(*sums2)
    outer = outer.astype(half)
    grad_in, keep1, keep2 = back_stage(
        back1, back2, up_left, after=(outer,), carry=(sums1[0], sums2[0])
    )
    outer = share(outer, False) * factor
    outer = outer.reshape(2, -1, ROWS, BLK_HID)
    grads = [
        (factor * add(keep, got)).reshape(2, -1, ROWS, BLK_HID)
        for keep, got in ((keep1, got1), (keep2, got2))
    ]
    grad_left_down, grad_right_up = [
        jnp.concatenate([g[k] for g in grads], axis=0) for k in range(2)
    ]
    rows4 = BLK_IN // (Z * Y * CORES)
    grad_left_up = outer[0].reshape(LOCAL, rows4, BLK_HID)
    grad_right_down = (
        outer[1].reshape(LOCAL // 4, ROWS, 4, BLK_IN).transpose(0, 2, 1, 3).reshape(LOCAL, ROWS, BLK_IN)
    )
    return grad_in, grad_left_up, grad_right_up, grad_left_down, grad_right_down


def solution(mesh):
    in_specs = (
        P("block", "dp"),
        P("block", "dp"),
        P("block", None, None),
        P("block", None, None),
        P("block", None, None),
        P("block", None, None),
    )
    out_specs = (
        P("block", "dp"),
        P("block", "dp", None),
        P("block", "dp", None),
        P("block", "dp", None),
        P("block", "dp", None),
    )
    return jax.shard_map(shards, mesh=mesh, in_specs=in_specs, out_specs=out_specs, check_vma=False)
```

```python
import jax
import jax.numpy as jnp
from jax import lax
from jax.experimental import pallas as pl
from jax.experimental.pallas import tpu as pltpu
from jax.sharding import PartitionSpec as P

BLK_IN = 128
BLK_HID = 512
SPREAD = 8
LOCAL = 8
PEERS = 8
PAIR = 2 * SPREAD
VMEM_LIMIT = 63 * 1024 * 1024
ROWS = 16
PAIRS = LOCAL // 2
CHUNKS = (1, 3)

half = jnp.bfloat16
single = jnp.float32
root_two_pi = 0.7978845608028654

Z, Y, CORES = 4, 4, 2


def dp_perm(dz, dy, dc):
    pairs = []
    for z in range(Z):
        for y in range(Y):
            for c in range(CORES):
                source = (z * Y + y) * CORES + c
                target = ((z + dz) % Z * Y + (y + dy) % Y) * CORES + (c + dc) % CORES
                pairs.append((source, target))
    return pairs


def gelu_parts(pre):
    inner = root_two_pi * (pre + 0.044715 * pre * pre * pre)
    curve = jnp.tanh(inner)
    value = 0.5 * pre * (1.0 + curve)
    slope = 0.5 * (1.0 + curve) + 0.5 * pre * (1.0 - curve * curve) * root_two_pi * (
        1.0 + 3.0 * 0.044715 * pre * pre
    )
    return value, slope


def dot(left, right, over_left, over_right):
    return lax.dot_general(
        left, right, (((over_left,), (over_right,)), ((), ())), preferred_element_type=single
    )


def spread_pair(first, second):
    tokens = first.shape[-1]
    parts = [r.reshape(BLK_HID // SPREAD, SPREAD, tokens) for r in (first, second)]
    return jnp.concatenate(parts, axis=1).astype(half)


def position():
    dp = lax.axis_index("dp")
    return lax.rem(dp, CORES), lax.rem(lax.div(dp, CORES), Y), lax.div(dp, CORES * Y)


def call(
    kernel, grid, in_specs, out_specs, out_shape, scratch=(), after=(), carry=(), vmem=VMEM_LIMIT
):
    first = len(in_specs)
    extra = len(after) + len(carry)
    outs = len(out_specs)
    untouched = pl.BlockSpec(memory_space=pl.ANY)

    def body(*refs):
        ends = first + extra + outs
        kernel(position(), *refs[:first], *refs[first + extra : ends], *refs[ends + len(carry) :])

    run = pl.pallas_call(
        body,
        grid=grid,
        in_specs=list(in_specs) + [untouched] * extra,
        out_specs=list(out_specs) + [untouched] * len(carry),
        scratch_shapes=list(scratch),
        out_shape=list(out_shape) + [jax.ShapeDtypeStruct(c.shape, c.dtype) for c in carry],
        input_output_aliases={first + len(after) + i: outs + i for i in range(len(carry))},
        compiler_params=pltpu.CompilerParams(vmem_limit_bytes=vmem),
    )
    return lambda *operands: run(*operands, *after, *carry)


def first_kernel(chunk, x_ref, g_ref, up_ref, down_ref, out_ref):
    start = 2 * sum(CHUNKS[:chunk])
    for pair in range(2):
        ups, downs = [], []
        for i in (2 * pair, 2 * pair + 1):
            rows = slice(i * BLK_IN, (i + 1) * BLK_IN)
            ups.append(dot(up_ref[i], x_ref[rows], 0, 0))
            downs.append(dot(down_ref[i], g_ref[rows], 1, 0))
        where = slice(pair * PAIR, (pair + 1) * PAIR)
        for slot, both in enumerate((ups, downs)):
            spread = spread_pair(*both).reshape(PEERS, LOCAL, PAIR, -1)
            out_ref[:, slot, :, where] = spread[:, start : start + 2 * CHUNKS[chunk]]


def first_stage(chunk, inputs, grad_out, up_left, down_right, **order):
    tokens = inputs.shape[1]
    n = CHUNKS[chunk]

    def kernel(me, *refs):
        first_kernel(chunk, *refs)

    (out,) = call(
        kernel,
        (PAIRS // 2,),
        [
            pl.BlockSpec((4 * BLK_IN, tokens), lambda p: (p, 0)),
            pl.BlockSpec((4 * BLK_IN, tokens), lambda p: (p, 0)),
            pl.BlockSpec((4, BLK_IN, BLK_HID), lambda p: (p, 0, 0)),
            pl.BlockSpec((4, BLK_HID, BLK_IN), lambda p: (p, 0, 0)),
        ],
        [pl.BlockSpec((PEERS, 2, 2 * n, 2 * PAIR, tokens), lambda p: (0, 0, 0, p, 0))],
        [jax.ShapeDtypeStruct((PEERS, 2, 2 * n, LOCAL * SPREAD, tokens), half)],
        **order,
    )(inputs, grad_out, up_left, down_right)
    return out


def place(me, held, own_ref, near_ref, far_ref, index):
    for ry in range(Y):
        for rz in range(Z):
            group = (lax.rem(me[2] + rz, Z) * Y + lax.rem(me[1] + ry, Y)) * CORES
            own_ref[(ry, rz) + index] = held[group + me[0]]
            other = held[group + 1 - me[0]]
            if ry == 0:
                near_ref[(0, rz) + index] = other
            else:
                far_ref[(ry - 1, rz) + index] = other


def middle_kernel(me, got_ref, up_ref, down_ref, back_ref, own_ref, near_ref, far_ref, held):
    lows, mids = [], []
    for i in range(2):
        v = got_ref[:, 0, i].reshape(BLK_HID, -1)
        f = got_ref[:, 1, i].reshape(BLK_HID, -1)
        up, down = up_ref[i], down_ref[i]
        value, slope = gelu_parts(dot(up, v, 0, 0))
        hidden = value.astype(half)
        lows.append(dot(down, hidden, 0, 0))
        held[0] = dot(hidden, f, 1, 1).astype(half).reshape(-1, ROWS, BLK_HID)
        place(me, held.at[0], own_ref, near_ref, far_ref, (0, i))
        back = (dot(down, f, 1, 0) * slope).astype(half)
        mids.append(dot(up, back, 1, 0))
        held[1] = dot(v, back, 1, 1).astype(half).reshape(-1, ROWS, BLK_HID)
        place(me, held.at[1], own_ref, near_ref, far_ref, (1, i))
    back_ref[:, 0] = spread_pair(*lows).reshape(PEERS, LOCAL, PAIR, -1)
    back_ref[:, 1] = spread_pair(*mids).reshape(PEERS, LOCAL, PAIR, -1)


def middle_stage(chunk, got, up_right, down_left, **order):
    tokens = got.shape[-1]
    pairs = CHUNKS[chunk]
    start = sum(CHUNKS[:chunk])
    sizes = (Y, 1, Y - 1)
    grads = [jax.ShapeDtypeStruct((n, Z, 2, 2 * pairs, ROWS, BLK_HID), half) for n in sizes]
    grads_specs = [
        pl.BlockSpec((n, Z, 2, 2, ROWS, BLK_HID), lambda p: (0, 0, 0, p, 0, 0)) for n in sizes
    ]
    weight = pl.BlockSpec((2, BLK_HID, BLK_HID), lambda p: (start + p, 0, 0))
    return call(
        middle_kernel,
        (pairs,),
        [
            pl.BlockSpec((PEERS, 2, 2, LOCAL * SPREAD, tokens), lambda p: (0, 0, p, 0, 0)),
            weight,
            weight,
        ],
        [
            pl.BlockSpec((PEERS, 2, LOCAL, PAIR, tokens), lambda p: (0, 0, 0, p, 0)),
            *grads_specs,
        ],
        [
            jax.ShapeDtypeStruct((PEERS, 2, LOCAL, pairs * PAIR, tokens), half),
            *grads,
        ],
        scratch=[pltpu.VMEM((2, BLK_HID // ROWS, ROWS, BLK_HID), half)],
        **order,
    )(got, up_right, down_left)


def features(one_ref, two_ref, slot, i):
    both = jnp.concatenate([one_ref[:, slot, i], two_ref[:, slot, i]], axis=1)
    return both.reshape(BLK_HID, -1)


def outer_kernel(me, one_ref, two_ref, x_ref, g_ref, own_ref, near_ref, far_ref, held, held_down):
    rows4 = BLK_IN // (Z * Y * CORES)
    evens, odds = [], []
    for i in range(4):
        rows = slice(i * BLK_IN, (i + 1) * BLK_IN)
        left = dot(x_ref[rows], features(one_ref, two_ref, 1, i), 1, 1)
        left = left.reshape(-1, 2 * rows4, BLK_HID)
        evens.append(left[:, :rows4])
        odds.append(left[:, rows4:])
        right = dot(features(one_ref, two_ref, 0, i), g_ref[rows], 1, 1).astype(half)
        held_down[:, :, i * BLK_IN : (i + 1) * BLK_IN] = right.reshape(-1, ROWS, BLK_IN)
    for core, parts in enumerate((evens, odds)):
        held[core] = jnp.concatenate(parts, axis=1).astype(half)
    for ry in range(Y):
        for z in range(Z):
            chip = z * Y + lax.rem(me[1] + ry, Y)
            own_ref[ry, z, 0, 0] = held[me[0], chip]
            own_ref[ry, z, 1, 0] = held_down[chip * CORES + me[0]]
            other_ref, at = (near_ref, 0) if ry == 0 else (far_ref, ry - 1)
            other_ref[at, z, 0, 0] = held[1 - me[0], chip]
            other_ref[at, z, 1, 0] = held_down[chip * CORES + 1 - me[0]]


def got_specs(tokens):
    return [
        pl.BlockSpec((PEERS, 2, 4, n * PAIR, tokens), lambda p: (0, 0, p, 0, 0)) for n in CHUNKS
    ]


def outer_stage(one, two, inputs, grad_out, **order):
    tokens = inputs.shape[1]
    groups = LOCAL // 4
    sizes = (Y, 1, Y - 1)
    grads = [jax.ShapeDtypeStruct((n, Z, 2, groups, ROWS, BLK_HID), half) for n in sizes]
    grads_specs = [
        pl.BlockSpec((n, Z, 2, 1, ROWS, BLK_HID), lambda p: (0, 0, 0, p, 0, 0)) for n in sizes
    ]
    feats = pl.BlockSpec((4 * BLK_IN, tokens), lambda p: (p, 0))
    return call(
        outer_kernel,
        (groups,),
        got_specs(tokens) + [feats, feats],
        grads_specs,
        grads,
        scratch=[
            pltpu.VMEM((CORES, Z * Y, ROWS, BLK_HID), half),
            pltpu.VMEM((Z * Y * CORES, ROWS, BLK_HID), half),
        ],
        **order,
    )(one, two, inputs, grad_out)


def back_kernel(me, one_ref, two_ref, up_ref, in_ref):
    for i in range(4):
        rows = slice(i * BLK_IN, (i + 1) * BLK_IN)
        in_ref[rows] = dot(up_ref[i], features(one_ref, two_ref, 1, i), 1, 0).astype(half)


def back_stage(one, two, up_left, **order):
    tokens = one.shape[-1]
    return call(
        back_kernel,
        (LOCAL // 4,),
        got_specs(tokens) + [pl.BlockSpec((4, BLK_IN, BLK_HID), lambda p: (p, 0, 0))],
        [pl.BlockSpec((4 * BLK_IN, tokens), lambda p: (p, 0))],
        [jax.ShapeDtypeStruct((LOCAL * BLK_IN, tokens), half)],
        **order,
    )(one, two, up_left)


def flat(array):
    return array.reshape(array.shape[0], Z, -1, ROWS, BLK_HID)


def core_step(own, near, far):
    own = flat(own)
    got = [lax.ppermute(flat(part), "dp", dp_perm(0, 0, 1)) for part in (far, near)]
    keep = own[0].astype(single) + got[1][0].astype(single)
    sends = [own[r + 1].astype(single) + got[0][r].astype(single) for r in range(Y - 1)]
    return keep, *[total.astype(half) for total in sends]


def gate(arrays, after=()):
    def kernel(me, out_ref):
        out_ref[...] = jnp.zeros_like(out_ref)

    return call(
        kernel,
        (1,),
        [],
        [pl.BlockSpec((8, 128), lambda p: (0, 0))],
        [jax.ShapeDtypeStruct((8, 128), single)],
        after=after,
        carry=arrays,
        vmem=1 << 20,
    )()[1:]


def add(keep, got):
    return keep + sum(part.astype(single) for part in got)


def line_step(keep, *sends):
    got = [lax.ppermute(s, "dp", dp_perm(0, r + 1, 0)) for r, s in enumerate(sends)]
    sums = [add(keep[r], [part[r] for part in got]) for r in range(Z)]
    return sums[0], *[total.astype(half) for total in sums[1:]]


def end_moves(keep, *sends):
    return [lax.ppermute(s, "dp", dp_perm(r + 1, 0, 0)) for r, s in enumerate(sends)]


def exchange(array):
    return lax.all_to_all(array, "block", split_axis=0, concat_axis=0, tiled=True)


def line_groups(of_y):
    spans = (Z, CORES) if of_y else (Y, CORES)
    groups = []
    for i in range(spans[0]):
        for c in range(CORES):
            lines = [(i, y) if of_y else (z, i) for y, z in zip(range(Y), range(Z))]
            groups.append([(z * Y + y) * CORES + c for z, y in lines])
    return groups


def share(array, of_y):
    got = lax.all_to_all(
        array, "dp", split_axis=0, concat_axis=0, tiled=True, axis_index_groups=line_groups(of_y)
    )
    return got.astype(single).sum(axis=0)


def shards(inputs, grad_out, up_left, up_right, down_left, down_right):
    tokens = inputs.shape[1]
    factor = float(tokens * lax.axis_size("dp")) ** (-0.5)

    operands = (inputs, grad_out, up_left, down_right)
    one = first_stage(0, *operands)
    two = first_stage(1, *operands, after=(one,))
    back1, *rows = middle_stage(0, exchange(one), up_right, down_left)
    sums1 = line_step(*core_step(*rows))
    (back1,) = gate([back1], sums1)
    back2, own, near, far, *sums1 = middle_stage(
        1, exchange(two), up_right, down_left, carry=sums1
    )
    sums2 = core_step(own, near, far)
    back1, back2 = exchange(back1), exchange(back2)
    got1 = end_moves(*sums1)
    own, near, far = outer_stage(
        back1, back2, inputs, grad_out, after=[*got1[::2], sums2[0]]
    )
    keep, *sends = core_step(own, near, far)
    gated = gate([*sends, *line_step(*sums2)])
    sends, sums2 = gated[: len(sends)], gated[len(sends) :]
    outer = add(keep, [lax.ppermute(s, "dp", dp_perm(0, r + 1, 0)) for r, s in enumerate(sends)])
    got2 = end_moves(*sums2)
    outer = outer.astype(half)
    grad_in, keep1, keep2 = back_stage(
        back1, back2, up_left, after=(outer,), carry=(sums1[0], sums2[0])
    )
    outer = share(outer, False) * factor
    outer = outer.reshape(2, -1, ROWS, BLK_HID)
    grads = [
        (factor * add(keep, got)).reshape(2, -1, ROWS, BLK_HID)
        for keep, got in ((keep1, got1), (keep2, got2))
    ]
    grad_left_down, grad_right_up = [
        jnp.concatenate([g[k] for g in grads], axis=0) for k in range(2)
    ]
    rows4 = BLK_IN // (Z * Y * CORES)
    grad_left_up = outer[0].reshape(LOCAL, rows4, BLK_HID)
    grad_right_down = (
        outer[1].reshape(LOCAL // 4, ROWS, 4, BLK_IN).transpose(0, 2, 1, 3).reshape(LOCAL, ROWS, BLK_IN)
    )
    return grad_in, grad_left_up, grad_right_up, grad_left_down, grad_right_down


def solution(mesh):
    in_specs = (
        P("block", "dp"),
        P("block", "dp"),
        P("block", None, None),
        P("block", None, None),
        P("block", None, None),
        P("block", None, None),
    )
    out_specs = (
        P("block", "dp"),
        P("block", "dp", None),
        P("block", "dp", None),
        P("block", "dp", None),
        P("block", "dp", None),
    )
    return jax.shard_map(shards, mesh=mesh, in_specs=in_specs, out_specs=out_specs, check_vma=False)
```

```python
import jax
import jax.numpy as jnp
from jax import lax
from jax.experimental import pallas as pl
from jax.experimental.pallas import tpu as pltpu
from jax.sharding import PartitionSpec as P

BLK_IN = 128
BLK_HID = 512
SPREAD = 8
LOCAL = 8
PEERS = 8
PAIR = 2 * SPREAD
VMEM_LIMIT = 63 * 1024 * 1024
ROWS = 16
PAIRS = LOCAL // 2
CHUNKS = (1, 3)

half = jnp.bfloat16
single = jnp.float32
root_two_pi = 0.7978845608028654

Z, Y, CORES = 4, 4, 2


def dp_perm(dz, dy, dc):
    pairs = []
    for z in range(Z):
        for y in range(Y):
            for c in range(CORES):
                source = (z * Y + y) * CORES + c
                target = ((z + dz) % Z * Y + (y + dy) % Y) * CORES + (c + dc) % CORES
                pairs.append((source, target))
    return pairs


def gelu_parts(pre):
    inner = root_two_pi * (pre + 0.044715 * pre * pre * pre)
    curve = jnp.tanh(inner)
    value = 0.5 * pre * (1.0 + curve)
    slope = 0.5 * (1.0 + curve) + 0.5 * pre * (1.0 - curve * curve) * root_two_pi * (
        1.0 + 3.0 * 0.044715 * pre * pre
    )
    return value, slope


def dot(left, right, over_left, over_right):
    return lax.dot_general(
        left, right, (((over_left,), (over_right,)), ((), ())), preferred_element_type=single
    )


def spread_pair(first, second):
    tokens = first.shape[-1]
    parts = [r.reshape(BLK_HID // SPREAD, SPREAD, tokens) for r in (first, second)]
    return jnp.concatenate(parts, axis=1).astype(half)


def position():
    dp = lax.axis_index("dp")
    return lax.rem(dp, CORES), lax.rem(lax.div(dp, CORES), Y), lax.div(dp, CORES * Y)


def call(
    kernel, grid, in_specs, out_specs, out_shape, scratch=(), after=(), carry=(), vmem=VMEM_LIMIT
):
    first = len(in_specs)
    extra = len(after) + len(carry)
    outs = len(out_specs)
    untouched = pl.BlockSpec(memory_space=pl.ANY)

    def body(*refs):
        ends = first + extra + outs
        kernel(position(), *refs[:first], *refs[first + extra : ends], *refs[ends + len(carry) :])

    run = pl.pallas_call(
        body,
        grid=grid,
        in_specs=list(in_specs) + [untouched] * extra,
        out_specs=list(out_specs) + [untouched] * len(carry),
        scratch_shapes=list(scratch),
        out_shape=list(out_shape) + [jax.ShapeDtypeStruct(c.shape, c.dtype) for c in carry],
        input_output_aliases={first + len(after) + i: outs + i for i in range(len(carry))},
        compiler_params=pltpu.CompilerParams(vmem_limit_bytes=vmem),
    )
    return lambda *operands: run(*operands, *after, *carry)


def first_kernel(chunk, x_ref, g_ref, up_ref, down_ref, out_ref):
    start = 2 * sum(CHUNKS[:chunk])
    for pair in range(2):
        ups, downs = [], []
        for i in (2 * pair, 2 * pair + 1):
            rows = slice(i * BLK_IN, (i + 1) * BLK_IN)
            ups.append(dot(up_ref[i], x_ref[rows], 0, 0))
            downs.append(dot(down_ref[i], g_ref[rows], 1, 0))
        where = slice(pair * PAIR, (pair + 1) * PAIR)
        for slot, both in enumerate((ups, downs)):
            spread = spread_pair(*both).reshape(PEERS, LOCAL, PAIR, -1)
            out_ref[:, slot, :, where] = spread[:, start : start + 2 * CHUNKS[chunk]]


def first_stage(chunk, inputs, grad_out, up_left, down_right, **order):
    tokens = inputs.shape[1]
    n = CHUNKS[chunk]

    def kernel(me, *refs):
        first_kernel(chunk, *refs)

    (out,) = call(
        kernel,
        (PAIRS // 2,),
        [
            pl.BlockSpec((4 * BLK_IN, tokens), lambda p: (p, 0)),
            pl.BlockSpec((4 * BLK_IN, tokens), lambda p: (p, 0)),
            pl.BlockSpec((4, BLK_IN, BLK_HID), lambda p: (p, 0, 0)),
            pl.BlockSpec((4, BLK_HID, BLK_IN), lambda p: (p, 0, 0)),
        ],
        [pl.BlockSpec((PEERS, 2, 2 * n, 2 * PAIR, tokens), lambda p: (0, 0, 0, p, 0))],
        [jax.ShapeDtypeStruct((PEERS, 2, 2 * n, LOCAL * SPREAD, tokens), half)],
        **order,
    )(inputs, grad_out, up_left, down_right)
    return out


def place(me, held, own_ref, near_ref, far_ref, index):
    for ry in range(Y):
        for rz in range(Z):
            group = (lax.rem(me[2] + rz, Z) * Y + lax.rem(me[1] + ry, Y)) * CORES
            own_ref[(ry, rz) + index] = held[group + me[0]]
            other = held[group + 1 - me[0]]
            if ry == 0:
                near_ref[(0, rz) + index] = other
            else:
                far_ref[(ry - 1, rz) + index] = other


def middle_kernel(me, got_ref, up_ref, down_ref, back_ref, own_ref, near_ref, far_ref, held):
    lows, mids = [], []
    for i in range(2):
        v = got_ref[:, 0, i].reshape(BLK_HID, -1)
        f = got_ref[:, 1, i].reshape(BLK_HID, -1)
        up, down = up_ref[i], down_ref[i]
        value, slope = gelu_parts(dot(up, v, 0, 0))
        hidden = value.astype(half)
        lows.append(dot(down, hidden, 0, 0))
        held[0] = dot(hidden, f, 1, 1).astype(half).reshape(-1, ROWS, BLK_HID)
        place(me, held.at[0], own_ref, near_ref, far_ref, (0, i))
        back = (dot(down, f, 1, 0) * slope).astype(half)
        mids.append(dot(up, back, 1, 0))
        held[1] = dot(v, back, 1, 1).astype(half).reshape(-1, ROWS, BLK_HID)
        place(me, held.at[1], own_ref, near_ref, far_ref, (1, i))
    back_ref[:, 0] = spread_pair(*lows).reshape(PEERS, LOCAL, PAIR, -1)
    back_ref[:, 1] = spread_pair(*mids).reshape(PEERS, LOCAL, PAIR, -1)


def middle_stage(chunk, got, up_right, down_left, **order):
    tokens = got.shape[-1]
    pairs = CHUNKS[chunk]
    start = sum(CHUNKS[:chunk])
    sizes = (Y, 1, Y - 1)
    grads = [jax.ShapeDtypeStruct((n, Z, 2, 2 * pairs, ROWS, BLK_HID), half) for n in sizes]
    grads_specs = [
        pl.BlockSpec((n, Z, 2, 2, ROWS, BLK_HID), lambda p: (0, 0, 0, p, 0, 0)) for n in sizes
    ]
    weight = pl.BlockSpec((2, BLK_HID, BLK_HID), lambda p: (start + p, 0, 0))
    return call(
        middle_kernel,
        (pairs,),
        [
            pl.BlockSpec((PEERS, 2, 2, LOCAL * SPREAD, tokens), lambda p: (0, 0, p, 0, 0)),
            weight,
            weight,
        ],
        [
            pl.BlockSpec((PEERS, 2, LOCAL, PAIR, tokens), lambda p: (0, 0, 0, p, 0)),
            *grads_specs,
        ],
        [
            jax.ShapeDtypeStruct((PEERS, 2, LOCAL, pairs * PAIR, tokens), half),
            *grads,
        ],
        scratch=[pltpu.VMEM((2, BLK_HID // ROWS, ROWS, BLK_HID), half)],
        **order,
    )(got, up_right, down_left)


def features(one_ref, two_ref, slot, i):
    both = jnp.concatenate([one_ref[:, slot, i], two_ref[:, slot, i]], axis=1)
    return both.reshape(BLK_HID, -1)


def outer_kernel(me, one_ref, two_ref, x_ref, g_ref, own_ref, near_ref, far_ref, held, held_down):
    rows4 = BLK_IN // (Z * Y * CORES)
    evens, odds = [], []
    for i in range(4):
        rows = slice(i * BLK_IN, (i + 1) * BLK_IN)
        left = dot(x_ref[rows], features(one_ref, two_ref, 1, i), 1, 1)
        left = left.reshape(-1, 2 * rows4, BLK_HID)
        evens.append(left[:, :rows4])
        odds.append(left[:, rows4:])
        right = dot(features(one_ref, two_ref, 0, i), g_ref[rows], 1, 1).astype(half)
        held_down[:, :, i * BLK_IN : (i + 1) * BLK_IN] = right.reshape(-1, ROWS, BLK_IN)
    for core, parts in enumerate((evens, odds)):
        held[core] = jnp.concatenate(parts, axis=1).astype(half)
    for ry in range(Y):
        for z in range(Z):
            chip = z * Y + lax.rem(me[1] + ry, Y)
            own_ref[ry, z, 0, 0] = held[me[0], chip]
            own_ref[ry, z, 1, 0] = held_down[chip * CORES + me[0]]
            other_ref, at = (near_ref, 0) if ry == 0 else (far_ref, ry - 1)
            other_ref[at, z, 0, 0] = held[1 - me[0], chip]
            other_ref[at, z, 1, 0] = held_down[chip * CORES + 1 - me[0]]


def got_specs(tokens):
    return [
        pl.BlockSpec((PEERS, 2, 4, n * PAIR, tokens), lambda p: (0, 0, p, 0, 0)) for n in CHUNKS
    ]


def outer_stage(one, two, inputs, grad_out, **order):
    tokens = inputs.shape[1]
    groups = LOCAL // 4
    sizes = (Y, 1, Y - 1)
    grads = [jax.ShapeDtypeStruct((n, Z, 2, groups, ROWS, BLK_HID), half) for n in sizes]
    grads_specs = [
        pl.BlockSpec((n, Z, 2, 1, ROWS, BLK_HID), lambda p: (0, 0, 0, p, 0, 0)) for n in sizes
    ]
    feats = pl.BlockSpec((4 * BLK_IN, tokens), lambda p: (p, 0))
    return call(
        outer_kernel,
        (groups,),
        got_specs(tokens) + [feats, feats],
        grads_specs,
        grads,
        scratch=[
            pltpu.VMEM((CORES, Z * Y, ROWS, BLK_HID), half),
            pltpu.VMEM((Z * Y * CORES, ROWS, BLK_HID), half),
        ],
        **order,
    )(one, two, inputs, grad_out)


def back_kernel(me, one_ref, two_ref, up_ref, in_ref):
    for i in range(4):
        rows = slice(i * BLK_IN, (i + 1) * BLK_IN)
        in_ref[rows] = dot(up_ref[i], features(one_ref, two_ref, 1, i), 1, 0).astype(half)


def back_stage(one, two, up_left, **order):
    tokens = one.shape[-1]
    return call(
        back_kernel,
        (LOCAL // 4,),
        got_specs(tokens) + [pl.BlockSpec((4, BLK_IN, BLK_HID), lambda p: (p, 0, 0))],
        [pl.BlockSpec((4 * BLK_IN, tokens), lambda p: (p, 0))],
        [jax.ShapeDtypeStruct((LOCAL * BLK_IN, tokens), half)],
        **order,
    )(one, two, up_left)


def flat(array):
    return array.reshape(array.shape[0], Z, -1, ROWS, BLK_HID)


def core_step(own, near, far):
    own = flat(own)
    got = [lax.ppermute(flat(part), "dp", dp_perm(0, 0, 1)) for part in (far, near)]
    keep = own[0].astype(single) + got[1][0].astype(single)
    sends = [own[r + 1].astype(single) + got[0][r].astype(single) for r in range(Y - 1)]
    return keep, *[total.astype(half) for total in sends]


def gate(arrays, after=()):
    def kernel(me, out_ref):
        out_ref[...] = jnp.zeros_like(out_ref)

    return call(
        kernel,
        (1,),
        [],
        [pl.BlockSpec((8, 128), lambda p: (0, 0))],
        [jax.ShapeDtypeStruct((8, 128), single)],
        after=after,
        carry=arrays,
        vmem=1 << 20,
    )()[1:]


def add(keep, got):
    return keep + sum(part.astype(single) for part in got)


def line_step(keep, *sends):
    got = [lax.ppermute(s, "dp", dp_perm(0, r + 1, 0)) for r, s in enumerate(sends)]
    sums = [add(keep[r], [part[r] for part in got]) for r in range(Z)]
    return sums[0], *[total.astype(half) for total in sums[1:]]


def end_moves(keep, *sends):
    return [lax.ppermute(s, "dp", dp_perm(r + 1, 0, 0)) for r, s in enumerate(sends)]


def exchange(array):
    return lax.all_to_all(array, "block", split_axis=0, concat_axis=0, tiled=True)


def line_groups(of_y):
    spans = (Z, CORES) if of_y else (Y, CORES)
    groups = []
    for i in range(spans[0]):
        for c in range(CORES):
            lines = [(i, y) if of_y else (z, i) for y, z in zip(range(Y), range(Z))]
            groups.append([(z * Y + y) * CORES + c for z, y in lines])
    return groups


def share(array, of_y):
    got = lax.all_to_all(
        array, "dp", split_axis=0, concat_axis=0, tiled=True, axis_index_groups=line_groups(of_y)
    )
    return got.astype(single).sum(axis=0)


def shards(inputs, grad_out, up_left, up_right, down_left, down_right):
    tokens = inputs.shape[1]
    factor = float(tokens * lax.axis_size("dp")) ** (-0.5)

    operands = (inputs, grad_out, up_left, down_right)
    one = first_stage(0, *operands)
    two = first_stage(1, *operands, after=(one,))
    back1, *rows = middle_stage(0, exchange(one), up_right, down_left)
    sums1 = line_step(*core_step(*rows))
    (back1,) = gate([back1], sums1)
    back2, own, near, far, *sums1 = middle_stage(
        1, exchange(two), up_right, down_left, carry=sums1
    )
    sums2 = core_step(own, near, far)
    back1, back2 = exchange(back1), exchange(back2)
    got1 = [lax.ppermute(sums1[r], "dp", dp_perm(r, 0, 0)) for r in (1, 3)]
    own, near, far = outer_stage(
        back1, back2, inputs, grad_out, after=[*got1, sums2[0]]
    )
    keep, *sends = core_step(own, near, far)
    gated = gate([*sends, *line_step(*sums2)])
    sends, sums2 = gated[: len(sends)], gated[len(sends) :]
    outer = add(keep, [lax.ppermute(s, "dp", dp_perm(0, r + 1, 0)) for r, s in enumerate(sends)])
    got2 = end_moves(*sums2)
    outer = outer.astype(half)
    grad_in, keep1, keep2, late = back_stage(
        back1, back2, up_left, after=(outer,), carry=(sums1[0], sums2[0], sums1[2])
    )
    got1.append(lax.ppermute(late, "dp", dp_perm(2, 0, 0)))
    outer = share(outer, False) * factor
    outer = outer.reshape(2, -1, ROWS, BLK_HID)
    grads = [
        (factor * add(keep, got)).reshape(2, -1, ROWS, BLK_HID)
        for keep, got in ((keep1, got1), (keep2, got2))
    ]
    grad_left_down, grad_right_up = [
        jnp.concatenate([g[k] for g in grads], axis=0) for k in range(2)
    ]
    rows4 = BLK_IN // (Z * Y * CORES)
    grad_left_up = outer[0].reshape(LOCAL, rows4, BLK_HID)
    grad_right_down = (
        outer[1].reshape(LOCAL // 4, ROWS, 4, BLK_IN).transpose(0, 2, 1, 3).reshape(LOCAL, ROWS, BLK_IN)
    )
    return grad_in, grad_left_up, grad_right_up, grad_left_down, grad_right_down


def solution(mesh):
    in_specs = (
        P("block", "dp"),
        P("block", "dp"),
        P("block", None, None),
        P("block", None, None),
        P("block", None, None),
        P("block", None, None),
    )
    out_specs = (
        P("block", "dp"),
        P("block", "dp", None),
        P("block", "dp", None),
        P("block", "dp", None),
        P("block", "dp", None),
    )
    return jax.shard_map(shards, mesh=mesh, in_specs=in_specs, out_specs=out_specs, check_vma=False)
```
